32 devices in a mesh: section: 2 (over core), row: 4 (over z), col: 4 (over y, x).
Axes of the slice: x: 2, y: 2, z: 4, core: 2. Of those that a mesh axis runs over, the one named last changes fastest.
Arguments:
- acts: bfloat16 [2, 4096, 768], P(None, ('row', 'col')), may hold values from -6 to 6
- segments: int32 [2, 4096], P(None, 'row'), may hold values from 0 to 2, as said below
- norm_gains: float32 [2, 2, 768], P('section'), may hold values from 0.5 to 1.5
- norm_biases: float32 [2, 2, 768], P('section'), may hold values from -1.2 to 1.2
- w_qkv: bfloat16 [2, 768, 2304], P('section', 'row', 'col'), may hold values from -0.21875 to 0.21875
- w_out: bfloat16 [2, 768, 768], P('section', 'col', 'row'), may hold values from -2 to 2
- w_up: bfloat16 [2, 768, 3072], P('section', 'row', 'col'), may hold values from -0.21875 to 0.21875
- w_down: bfloat16 [2, 3072, 768], P('section', 'col', 'row'), may hold values from -0.109375 to 0.109375
- out_grad: bfloat16 [2, 4096, 768], P(None, ('row', 'col')), may hold values from -6 to 6
Outputs:
- layer_outputs: bfloat16 [2, 2, 4096, 768], P('section', None, ('row', 'col'))
- input_grads: bfloat16 [2, 2, 4096, 768], P('section', None, ('row', 'col'))
- grad_gains: float32 [2, 2, 768], P('section')
- grad_biases: float32 [2, 768], P('section')
- grad_mlp_biases: float32 [2, 768], P('section')
- grad_qkv: float32 [2, 768, 2304], P('section', 'row', 'col')
- grad_out: float32 [2, 768, 768], P('section', 'col', 'row')
- grad_up: float32 [2, 768, 3072], P('section', 'row', 'col')
- grad_down: float32 [2, 3072, 768], P('section', 'col', 'row')
The draws below stay inside these ranges and needn't reach their ends.
Inputs may be any that keep to these rules, and one draw needn't show every extreme that they name: `segments`: in every sequence of 1024 tokens the segment numbers start at 0, never fall and rise by one at each new document; a sequence holds one to three documents of 200 to 1024 tokens.
All inputs are finite; a program needn't handle non-finite values.
Results may differ from the reference program's by a relative error of at most 0.019.
Values may be sent and summed in bfloat16 or wider, within the bound.
A program may use at most 128 MiB of HBM per device.

```python
import jax
import jax.numpy as jnp
from jax import lax

D = 768
H = 12
FF = 3072
HD = 64
ROT = 16
SEQ_LEN = 1024
MICRO = 2
LAYERS = 2
TOKENS = 4096


def draw_segments(key, part):
    key = jax.random.fold_in(key, 7)
    least_len = SEQ_LEN * 25 // 128
    spare_len = (SEQ_LEN - 3 * least_len) // 2 + 1
    key_one, key_two, key_three, key_four = jax.random.split(key, 4)
    seq_count = MICRO * (TOKENS // SEQ_LEN)
    first_cut = least_len + jax.random.randint(key_one, (seq_count, 1), 0, spare_len)
    second_cut = first_cut + least_len + jax.random.randint(key_two, (seq_count, 1), 0, spare_len)
    keep_first = jax.random.randint(key_three, (seq_count, 1), 0, 2)
    keep_second = jax.random.randint(key_four, (seq_count, 1), 0, 2)
    seq_index = jnp.arange(seq_count)[:, None]
    first_cut = jnp.where(seq_index == 0, least_len, first_cut)
    keep_first = jnp.where(seq_index == 0, 1, jnp.where(seq_index == 1, 0, keep_first))
    keep_second = jnp.where(seq_index == 0, 1, jnp.where(seq_index == 1, 0, keep_second))
    places = jnp.arange(SEQ_LEN)[None, :]
    numbers = (places >= first_cut).astype(jnp.int32) * keep_first + (places >= second_cut).astype(jnp.int32) * keep_second
    return numbers.reshape(MICRO, TOKENS).astype(jnp.int32)


def levels(rng, dims, cuts, low, largest):
    gain, own = 1.0, jax.random.fold_in(rng, 6)
    for dim, parts in cuts:
        heights = jnp.exp(jax.random.uniform(jax.random.fold_in(own, dim), (parts,), jnp.float32, low / len(cuts), largest / len(cuts)))
        gain = gain * jnp.repeat(heights, dims[dim] // parts).reshape([-1 if axis == dim else 1 for axis in range(len(dims))])
    return gain


def centred(stream_key, dims, scale, bound, cuts=(), held_as=jnp.bfloat16):
    values = scale * jax.random.normal(stream_key, dims, jnp.float32)
    if cuts:
        values = values * levels(stream_key, dims, cuts, -0.22, 0.18)
    return jnp.clip(values, -bound, bound).astype(held_as)


def setup_inputs(seed: int = 0) -> dict:
    seeds = jax.random.split(jax.random.key(seed), 10)
    acts = centred(seeds[0], (MICRO, TOKENS, D), 1.0, 6.0, ((1, 16),))
    segments = draw_segments(jax.random.fold_in(seeds[9], 71), 0)
    norm_gains = jnp.clip(1.0 + 0.1 * jax.random.normal(seeds[2], (LAYERS, 2, D), jnp.float32), 0.5, 1.5)
    norm_biases = centred(seeds[3], (LAYERS, 2, D), 0.2, 1.2, ((0, 2),), jnp.float32)
    w_qkv = centred(seeds[4], (LAYERS, D, 3 * D), D ** -0.5, 0.21875, ((0, 2), (1, 4), (2, 4)))
    w_out = centred(seeds[5], (LAYERS, D, D), (max(D // 96, 1)) ** -0.5, 2.0, ((0, 2), (1, 4), (2, 4)))
    w_up = centred(seeds[6], (LAYERS, D, FF), D ** -0.5, 0.21875, ((0, 2), (1, 4), (2, 4)))
    w_down = centred(seeds[7], (LAYERS, FF, D), FF ** -0.5, 0.109375, ((0, 2), (1, 4), (2, 4)))
    out_grad = centred(seeds[8], (MICRO, TOKENS, D), 1.0, 6.0, ((1, 16),))
    return dict(acts=acts, segments=segments, norm_gains=norm_gains, norm_biases=norm_biases, w_qkv=w_qkv, w_out=w_out, w_up=w_up, w_down=w_down, out_grad=out_grad)


@jax.custom_vjp
def low(v):
    return lax.optimization_barrier(v.astype(jnp.bfloat16)).astype(jnp.float32)

@jax.custom_vjp
def low_back(v):
    return v

def low_keep(v):
    return (low(v), None)

def low_pass(kept, grad):
    return (grad,)

def back_keep(v):
    return (v, None)

def back_low(kept, grad):
    return (low(grad),)
low.defvjp(low_keep, low_pass)
low_back.defvjp(back_keep, back_low)
EPSILON = 1e-05
HIGHEST = lax.Precision.HIGHEST

def product(left, right):
    return jnp.dot(left, right, precision=HIGHEST)

def normalize(inputs, gain_row, bias_row):
    centre = lax.optimization_barrier(jnp.mean(inputs, axis=-1, keepdims=True))
    spread = lax.optimization_barrier(jnp.mean(inputs * inputs, axis=-1, keepdims=True)) - centre * centre
    return (inputs - centre) * lax.rsqrt(spread + EPSILON) * gain_row + bias_row

def rotary_tables(length):
    places = jnp.arange(length).astype(jnp.float32)
    inverse = 10000.0 ** (-jnp.arange(0, ROT, 2).astype(jnp.float32) / ROT)
    angles = places[:, None] * inverse[None, :]
    angles = jnp.concatenate([angles, angles], axis=-1)[:, None, :]
    return (jnp.cos(angles), jnp.sin(angles))

def rotate(heads, cosine, sine):
    turned_part = heads[..., :ROT]
    half_rot = ROT // 2
    swapped = jnp.concatenate([-turned_part[..., half_rot:], turned_part[..., :half_rot]], axis=-1)
    return jnp.concatenate([turned_part * cosine + swapped * sine, heads[..., ROT:]], axis=-1)

def layer(inputs, gains, biases, w_qkv, w_out, w_up, w_down, segment, cosine, sine):
    length = inputs.shape[0]
    attn_in = low(normalize(inputs, gains[0], biases[0]))
    mlp_in = low(normalize(inputs, gains[1], biases[1]))
    packed = low_back(product(attn_in, w_qkv)).reshape(length, H, 3, HD)
    queries = low(rotate(packed[:, :, 0], cosine, sine))
    keys_all = low(rotate(packed[:, :, 1], cosine, sine))
    values = low(packed[:, :, 2])
    scores = low_back(jnp.einsum('qhd,khd->hqk', queries, keys_all, precision=HIGHEST) * HD ** (-0.5))
    places = jnp.arange(length)
    allowed = (segment[:, None] == segment[None, :]) & (places[:, None] >= places[None, :])
    scores = jnp.where(allowed[None], scores, -1000000000.0)
    biggest = lax.optimization_barrier(jnp.max(scores, axis=-1, keepdims=True))
    raised = jnp.exp(scores - biggest)
    softened = raised / lax.optimization_barrier(jnp.sum(raised, axis=-1, keepdims=True))
    context = jnp.einsum('hqk,khd->qhd', low(softened), values, precision=HIGHEST)
    context = low(low_back(context)).reshape(length, D)
    hidden = low_back(product(mlp_in, w_up))
    active = low(jax.nn.gelu(hidden, approximate=False))
    return inputs + product(context, w_out) + product(active, w_down)

def network(first_in, relay_in, gains, biases, w_qkv, w_out, w_up, w_down, segment):
    cosine, sine = rotary_tables(first_in.shape[0])
    middle = low(layer(first_in, gains[0], biases[0], w_qkv[0], w_out[0], w_up[0], w_down[0], segment, cosine, sine))
    passed = low_back(middle + relay_in)
    last_out = layer(passed, gains[1], biases[1], w_qkv[1], w_out[1], w_up[1], w_down[1], segment, cosine, sine)
    return (last_out, middle)

def reference(acts, segments, norm_gains, norm_biases, w_qkv, w_out, w_up, w_down, out_grad):
    params = tuple((member.astype(jnp.float32) for member in (norm_gains, norm_biases, w_qkv, w_out, w_up, w_down)))
    seq_inputs = acts.reshape(-1, SEQ_LEN, D).astype(jnp.float32)
    seq_grads = out_grad.reshape(-1, SEQ_LEN, D).astype(jnp.float32)
    seq_segments = segments.reshape(-1, SEQ_LEN)

    def one_sequence(totals, pieces):
        first_in, cotangent, segment = pieces
        relay_in = jnp.zeros_like(first_in)

        def run_net(first_value, relay_value, *weight_list):
            return network(first_value, relay_value, *weight_list, segment)
        last_out, pullback, middle = jax.vjp(run_net, first_in, relay_in, *params, has_aux=True)
        gradients = pullback(cotangent)
        totals = tuple((running + fresh_grad for running, fresh_grad in zip(totals, gradients[2:])))
        return (totals, (middle.astype(jnp.bfloat16), last_out.astype(jnp.bfloat16), gradients[0].astype(jnp.bfloat16), gradients[1].astype(jnp.bfloat16)))
    initial = tuple((jnp.zeros_like(member) for member in params))
    totals, outs_seq = lax.scan(one_sequence, initial, (seq_inputs, seq_grads, seq_segments))
    middles, finals, first_grads, relay_grads = outs_seq
    layer_outputs = jnp.stack([middles.reshape(MICRO, TOKENS, D), finals.reshape(MICRO, TOKENS, D)])
    input_grads = jnp.stack([first_grads.reshape(MICRO, TOKENS, D), relay_grads.reshape(MICRO, TOKENS, D)])
    return (layer_outputs, input_grads, totals[0], totals[1][:, 0], totals[1][:, 1], totals[2], totals[3], totals[4], totals[5])
```

```python
from functools import partial

import jax
import jax.numpy as jnp
from jax import lax
from jax.sharding import PartitionSpec as P

HD = 64
ROT = 16
EPSILON = 1e-05
F32 = jnp.float32
BF16 = jnp.bfloat16


def contract(left, right, left_dim, right_dim):
    return lax.dot_general(
        left, right, (((left_dim,), (right_dim,)), ((), ())), preferred_element_type=F32
    )


def col_gather(piece):
    n = lax.axis_size("col")
    me = lax.axis_index("col")
    rows = piece.shape[0]
    pieces = [piece]
    for k in range(1, n):
        pieces.append(lax.ppermute(piece, "col", [(i, (i + k) % n) for i in range(n)]))
    whole = jnp.zeros((rows * n, piece.shape[1]), piece.dtype)
    for k in range(n):
        whole = lax.dynamic_update_slice(whole, pieces[k], (lax.rem(me - k + n, n) * rows, 0))
    return whole


def col_scatter(total):
    n = lax.axis_size("col")
    me = lax.axis_index("col")
    rows = total.shape[0] // n
    width = total.shape[1]
    low = total.astype(BF16)

    def chunk(source, k):
        return lax.dynamic_slice(source, (lax.rem(me + k, n) * rows, 0), (rows, width))

    arrived = [
        lax.ppermute(chunk(low, k), "col", [(i, (i + k) % n) for i in range(n)])
        for k in range(1, n)
    ]
    result = chunk(total, 0)
    for piece in arrived:
        result = result + piece.astype(F32)
    return result


def pairs_of(section, shift, n):
    return [(section * n + i, section * n + (i + shift) % n) for i in range(n)]


def row_gather(piece, axis, section):
    n = lax.axis_size("row")
    if n > 8:
        whole = lax.all_gather(piece, "row", axis=axis, tiled=True)
    else:
        me = lax.axis_index("row")
        size = piece.shape[axis]
        shape = tuple(d * n if a == axis else d for a, d in enumerate(piece.shape))
        pieces = [piece]
        for k in range(1, n):
            pieces.append(lax.ppermute(piece, ("section", "row"), pairs_of(section, k, n)))
        whole = jnp.zeros(shape, piece.dtype)
        for k in range(n):
            at = lax.rem(me - k + n, n) * size
            whole = lax.dynamic_update_slice(whole, pieces[k], (at, 0) if axis == 0 else (0, at))
    other = lax.ppermute(whole, "section", [(section, 1 - section)])
    return jnp.where(lax.axis_index("section") == section, whole, other)


def row_scatter(term, axis, section):
    n = lax.axis_size("row")
    other = lax.ppermute(term.astype(BF16), "section", [(1 - section, section)])
    total = term + other.astype(F32)
    if n > 8:
        return lax.psum_scatter(
            total.astype(BF16), "row", scatter_dimension=axis, tiled=True
        ).astype(F32)
    me = lax.axis_index("row")
    sizes = tuple(d // n if a == axis else d for a, d in enumerate(term.shape))

    def chunk(k):
        at = lax.rem(me + k, n) * sizes[axis]
        return lax.dynamic_slice(total, (at, 0) if axis == 0 else (0, at), sizes)

    arrived = [
        lax.ppermute(chunk(k).astype(BF16), ("section", "row"), pairs_of(section, k, n))
        for k in range(1, n)
    ]
    result = chunk(0)
    for piece in arrived:
        result = result + piece.astype(F32)
    return result


def rotary_tables(length, heads):
    places = jnp.arange(length).astype(F32)
    inverse = 10000.0 ** (-jnp.arange(0, ROT, 2).astype(F32) / ROT)
    angles = places[:, None] * inverse[None, :]
    cosine, sine = jnp.cos(angles), jnp.sin(angles)
    half = ROT // 2
    ones = jnp.ones((length, HD - ROT), F32)
    zeros = jnp.zeros((length, HD - ROT), F32)
    nil = jnp.zeros((length, half), F32)
    cos_one = jnp.concatenate([cosine, cosine, ones], axis=1)
    ahead_one = jnp.concatenate([-sine, nil, zeros], axis=1)
    behind_one = jnp.concatenate([nil, sine, zeros], axis=1)
    flat = jnp.zeros((length, HD), F32)

    def full(one, last):
        return jnp.tile(jnp.concatenate([one, one, last], axis=1), (1, heads))

    return full(cos_one, flat + 1.0), full(ahead_one, flat), full(behind_one, flat)


def shifted(array, by):
    return jnp.roll(array, by, axis=1)


def rotate(packed, tables):
    cosine, ahead, behind = tables
    half = ROT // 2
    return packed * cosine + shifted(packed, -half) * ahead + shifted(packed, half) * behind


def rotate_back(grad, tables):
    cosine, ahead, behind = tables
    half = ROT // 2
    return grad * cosine + shifted(grad * ahead, half) + shifted(grad * behind, -half)


def scores_of(query_block, keys_all, segment, begin, stop):
    places = jnp.arange(stop)
    scores = jnp.einsum(
        "qhd,khd->hqk", query_block, keys_all[:stop], preferred_element_type=F32
    ) * HD ** (-0.5)
    allowed = (segment[begin:stop, None] == segment[None, :stop]) & (
        places[begin:, None] >= places[None, :]
    )
    return jnp.where(allowed[None], scores, -1000000000.0)


def split_heads(packed):
    length, width = packed.shape
    parts = packed.reshape(length, width // (3 * HD), 3, HD)
    return parts[:, :, 0], parts[:, :, 1], parts[:, :, 2]


def attention_forward(packed, segment):
    queries, keys_all, values = split_heads(packed)
    length = packed.shape[0]
    block = min(512, length)
    outputs, totals = [], []
    for begin in range(0, length, block):
        stop = begin + block
        scores = scores_of(queries[begin:stop], keys_all, segment, begin, stop)
        biggest = jnp.max(scores, axis=-1, keepdims=True)
        raised = jnp.exp(scores - biggest)
        summed = jnp.sum(raised, axis=-1, keepdims=True)
        softened = (raised / summed).astype(BF16)
        outputs.append(
            jnp.einsum("hqk,khd->qhd", softened, values[:stop], preferred_element_type=F32)
        )
        totals.append((biggest + jnp.log(summed))[..., 0])
    context = jnp.concatenate(outputs, axis=0).astype(BF16).reshape(length, -1)
    return context, jnp.concatenate(totals, axis=1)


def attention_backward(packed, segment, log_totals, context_grad):
    queries, keys_all, values = split_heads(packed)
    length, heads = queries.shape[:2]
    context_grad = context_grad.reshape(length, heads, HD)
    block = min(512, length)
    factor = HD ** (-0.5)
    key_grad = jnp.zeros(keys_all.shape, F32)
    value_grad = jnp.zeros(values.shape, F32)
    query_grads = []
    for begin in range(0, length, block):
        stop = begin + block
        query_block = queries[begin:stop]
        grad_block = context_grad[begin:stop]
        scores = scores_of(query_block, keys_all, segment, begin, stop)
        softened = jnp.exp(scores - log_totals[:, begin:stop, None])
        soft_grad = jnp.einsum(
            "qhd,khd->hqk", grad_block, values[:stop], preferred_element_type=F32
        )
        inner = jnp.sum(softened * soft_grad, axis=-1, keepdims=True)
        score_grad = (softened * (soft_grad - inner)).astype(BF16)
        query_grads.append(
            jnp.einsum("hqk,khd->qhd", score_grad, keys_all[:stop], preferred_element_type=F32)
            * factor
        )
        key_grad = key_grad.at[:stop].add(
            jnp.einsum("hqk,qhd->khd", score_grad, query_block, preferred_element_type=F32)
            * factor
        )
        value_grad = value_grad.at[:stop].add(
            jnp.einsum(
                "hqk,qhd->khd", softened.astype(BF16), grad_block, preferred_element_type=F32
            )
        )
    grads = jnp.stack([jnp.concatenate(query_grads, axis=0), key_grad, value_grad], axis=2)
    return grads.reshape(length, -1)


def normalize(inputs):
    values_in = inputs.astype(F32)
    centre = jnp.mean(values_in, axis=1, keepdims=True)
    spread = jnp.mean(values_in * values_in, axis=1, keepdims=True) - centre * centre
    inverse = lax.rsqrt(spread + EPSILON)
    return (values_in - centre) * inverse, inverse


def layer_forward(own, inputs, segment, weights, gains, biases, tables):
    qkv, up, both = weights
    scaled = normalize(inputs)[0]
    attn_in = (scaled * gains[0] + biases[0]).astype(BF16)
    mlp_in = (scaled * gains[1] + biases[1]).astype(BF16)
    packed = rotate(jnp.dot(attn_in, qkv, preferred_element_type=F32), tables).astype(BF16)
    context, log_totals = attention_forward(packed, segment)
    hidden = jnp.dot(mlp_in, up, preferred_element_type=F32)
    active = jax.nn.gelu(hidden, approximate=False).astype(BF16)
    joined = jnp.concatenate([context, active], axis=1)
    branch = col_scatter(jnp.dot(joined, both, preferred_element_type=F32))
    result = (own.astype(F32) + branch).astype(BF16)
    return result, (own, inputs, attn_in, mlp_in, packed, log_totals, context)


def layer_backward(own_grad, grad_all, stored, segment, weights, gains, tables):
    qkv, up, both = weights
    own, inputs, attn_in, mlp_in, packed, log_totals, context = stored
    width = context.shape[1]
    joined_grad = contract(grad_all, both, 1, 1)
    context_grad = joined_grad[:, :width].astype(BF16)
    hidden = jnp.dot(mlp_in, up, preferred_element_type=F32)
    active, gelu_pull = jax.vjp(partial(jax.nn.gelu, approximate=False), hidden)
    hidden_grad = gelu_pull(joined_grad[:, width:])[0].astype(BF16)
    packed_grad = attention_backward(packed, segment, log_totals, context_grad)
    packed_grad = rotate_back(packed_grad, tables).astype(BF16)
    attn_grad = contract(packed_grad, qkv, 1, 1)
    mlp_grad = contract(hidden_grad, up, 1, 1)
    reduced = col_scatter(attn_grad * gains[0] + mlp_grad * gains[1])
    scaled_own, inverse_own = normalize(own)
    grad_mean = jnp.mean(reduced, axis=1, keepdims=True)
    cross_mean = jnp.mean(reduced * scaled_own, axis=1, keepdims=True)
    input_grad = own_grad.astype(F32) + inverse_own * (
        reduced - grad_mean - scaled_own * cross_mean
    )
    scaled = normalize(inputs)[0]
    small = jnp.stack(
        [
            jnp.sum(attn_grad * scaled, axis=0),
            jnp.sum(mlp_grad * scaled, axis=0),
            jnp.sum(attn_grad, axis=0),
            jnp.sum(mlp_grad, axis=0),
        ]
    )
    qkv_term = contract(attn_in, packed_grad, 0, 0)
    up_term = contract(mlp_in, hidden_grad, 0, 0)
    joined = jnp.concatenate([context, active.astype(BF16)], axis=1)
    both_term = contract(joined, grad_all, 0, 0)
    return input_grad.astype(BF16), (qkv_term, up_term, both_term), small


def butterfly(value, axis):
    n = lax.axis_size(axis)
    step = 1
    while step < n:
        value = value + lax.ppermute(value, axis, [(i, i ^ step) for i in range(n)])
        step *= 2
    return value


def body(acts, segments, norm_gains, norm_biases, w_qkv, w_out, w_up, w_down, out_grad):
    section = lax.axis_index("section")
    first = section == 0

    def mine(member):
        return lax.dynamic_index_in_dim(member, section, 0, keepdims=False)

    def swap(value):
        return lax.ppermute(value, "section", [(0, 1), (1, 0)])

    own = mine(acts)
    segment = mine(segments)
    last_grad = mine(out_grad)
    inputs = col_gather(own)
    joined_local = jnp.concatenate([w_out[0], w_down[0]], axis=0)
    weights = [
        (
            row_gather(w_qkv[0], 0, layer),
            row_gather(w_up[0], 0, layer),
            row_gather(joined_local, 1, layer),
        )
        for layer in range(2)
    ]
    norms = jnp.concatenate([norm_gains[0], norm_biases[0]], axis=0)
    norms_other = swap(norms)
    layer_norms = [
        jnp.where(first, norms, norms_other),
        jnp.where(first, norms_other, norms),
    ]
    gains = [member[:2] for member in layer_norms]
    biases = [member[2:] for member in layer_norms]
    tables = rotary_tables(inputs.shape[0], w_qkv.shape[2] // (3 * HD))

    middle, stored_first = layer_forward(
        own, inputs, segment, weights[0], gains[0], biases[0], tables
    )
    grad_all = col_gather(last_grad)
    inputs_last = col_gather(middle)
    last, stored_last = layer_forward(
        middle, inputs_last, segment, weights[1], gains[1], biases[1], tables
    )
    middle_grad, terms_last, small_last = layer_backward(
        last_grad, grad_all, stored_last, segment, weights[1], gains[1], tables
    )
    middle_grad_all = col_gather(middle_grad)
    totals_last = [row_scatter(t, a, 1) for t, a in zip(terms_last, (0, 0, 1))]
    first_grad, terms_first, small_first = layer_backward(
        middle_grad, middle_grad_all, stored_first, segment, weights[0], gains[0], tables
    )
    totals_first = [row_scatter(t, a, 0) for t, a in zip(terms_first, (0, 0, 1))]
    totals = [jnp.where(first, a, b) for a, b in zip(totals_first, totals_last)]

    small = jnp.where(first, small_first, small_last) + swap(
        jnp.where(first, small_last, small_first)
    )
    small = butterfly(butterfly(small, "col"), "row")

    def placed(of_first, of_last):
        kept = jnp.where(first, of_first, of_last)
        arrived = swap(jnp.where(first, of_last, of_first))
        return jnp.where(first, jnp.stack([kept, arrived]), jnp.stack([arrived, kept]))[None]

    split = w_out.shape[1]
    return (
        placed(middle, last),
        placed(first_grad, middle_grad),
        small[:2][None],
        small[2][None],
        small[3][None],
        totals[0][None],
        totals[2][:split][None],
        totals[1][None],
        totals[2][split:][None],
    )


def solution(mesh):
    placed = (
        P(None, ("row", "col"), None),
        P(None, "row"),
        P("section", None, None),
        P("section", None, None),
        P("section", "row", "col"),
        P("section", "col", "row"),
        P("section", "row", "col"),
        P("section", "col", "row"),
        P(None, ("row", "col"), None),
    )
    return jax.shard_map(
        body,
        mesh=mesh,
        in_specs=placed,
        out_specs=(
            P("section", None, ("row", "col"), None),
            P("section", None, ("row", "col"), None),
            P("section", None, None),
            P("section", None),
            P("section", None),
            P("section", "row", "col"),
            P("section", "col", "row"),
            P("section", "row", "col"),
            P("section", "col", "row"),
        ),
        check_vma=False,
    )
```

```python
from functools import partial

import jax
import jax.numpy as jnp
from jax import lax
from jax.experimental import pallas as pl
from jax.experimental.pallas import tpu as pltpu
from jax.sharding import PartitionSpec as P

HD = 64
ROT = 16
EPSILON = 1e-05
F32 = jnp.float32
BF16 = jnp.bfloat16


def contract(left, right, left_dim, right_dim):
    return lax.dot_general(
        left, right, (((left_dim,), (right_dim,)), ((), ())), preferred_element_type=F32
    )


def col_gather(piece):
    n = lax.axis_size("col")
    me = lax.axis_index("col")
    rows = piece.shape[0]
    pieces = [piece]
    for k in range(1, n):
        pieces.append(lax.ppermute(piece, "col", [(i, (i + k) % n) for i in range(n)]))
    whole = jnp.zeros((rows * n, piece.shape[1]), piece.dtype)
    for k in range(n):
        whole = lax.dynamic_update_slice(whole, pieces[k], (lax.rem(me - k + n, n) * rows, 0))
    return whole


def col_scatter(total):
    n = lax.axis_size("col")
    me = lax.axis_index("col")
    rows = total.shape[0] // n
    width = total.shape[1]
    low = total.astype(BF16)

    def chunk(source, k):
        return lax.dynamic_slice(source, (lax.rem(me + k, n) * rows, 0), (rows, width))

    arrived = [
        lax.ppermute(chunk(low, k), "col", [(i, (i + k) % n) for i in range(n)])
        for k in range(1, n)
    ]
    result = chunk(total, 0)
    for piece in arrived:
        result = result + piece.astype(F32)
    return result


def remote(source, target, send, recv, device):
    return pltpu.make_async_remote_copy(
        src_ref=source,
        dst_ref=target,
        send_sem=send,
        recv_sem=recv,
        device_id=device,
        device_id_type=pl.DeviceIdType.MESH,
    )


def greet(devices):
    barrier = pltpu.get_barrier_semaphore()
    for device in devices:
        pl.semaphore_signal(
            barrier, inc=1, device_id=device, device_id_type=pl.DeviceIdType.MESH
        )
    pl.semaphore_wait(barrier, len(devices))


def opening_kernel(nr, nc, *refs):
    pieces, outs = refs[:5], refs[5:10]
    local, row_send, row_recv, pair_send, pair_recv, col_send, col_recv = refs[10:]
    section, row, col = (lax.axis_index(a) for a in ("section", "row", "col"))
    partner = {"section": 1 - section}
    rows = [{"row": lax.rem(row + k, nr)} for k in range(1, nr)]
    cols = [{"col": lax.rem(col + k, nc)} for k in range(1, nc)]
    greet(rows + cols + [partner])
    weights, wholes = pieces[:3], outs[:3]
    tokens, gathered = pieces[3:], outs[3:]
    waits = []
    for k in range(1, nr):
        for j in range(3):
            copy = remote(
                weights[j],
                wholes[j].at[section, row],
                row_send.at[j * nr + k],
                row_recv.at[j * nr + k],
                rows[k - 1],
            )
            copy.start()
            waits.append(copy)
    for k in range(1, nc):
        for j in range(2):
            copy = remote(
                tokens[j],
                gathered[j].at[col],
                col_send.at[j * nc + k],
                col_recv.at[j * nc + k],
                cols[k - 1],
            )
            copy.start()
            waits.append(copy)
    locals_here = []
    passing = []
    for j in range(3):
        locals_here.append(
            pltpu.make_async_copy(weights[j], wholes[j].at[section, row], local.at[j])
        )
        passing.append(
            remote(
                weights[j],
                wholes[j].at[section, row],
                pair_send.at[j * nr],
                pair_recv.at[j * nr],
                partner,
            )
        )
    for j in range(2):
        locals_here.append(
            pltpu.make_async_copy(tokens[j], gathered[j].at[col], local.at[3 + j])
        )
    for copy in locals_here + passing:
        copy.start()
    for k in range(1, nr):
        origin = lax.rem(row - k + nr, nr)
        for j in range(3):
            waits[(k - 1) * 3 + j].wait_recv()
            copy = remote(
                wholes[j].at[section, origin],
                wholes[j].at[section, origin],
                pair_send.at[j * nr + k],
                pair_recv.at[j * nr + k],
                partner,
            )
            copy.start()
            passing.append(copy)
    for copy in locals_here:
        copy.wait()
    for at, copy in enumerate(waits):
        copy.wait_send()
        if at >= 3 * (nr - 1):
            copy.wait_recv()
    for copy in passing:
        copy.wait()


def opening(weights, tokens):
    nr, nc = lax.axis_size("row"), lax.axis_size("col")
    shapes = [jax.ShapeDtypeStruct((2, nr) + w.shape, w.dtype) for w in weights]
    shapes += [jax.ShapeDtypeStruct((nc,) + t.shape, t.dtype) for t in tokens]
    sems = [5, 3 * nr, 3 * nr, 3 * nr, 3 * nr, 2 * nc, 2 * nc]
    return pl.pallas_call(
        partial(opening_kernel, nr, nc),
        out_shape=shapes,
        in_specs=[pl.BlockSpec(memory_space=pl.ANY)] * 5,
        out_specs=[pl.BlockSpec(memory_space=pl.ANY)] * 5,
        scratch_shapes=[pltpu.SemaphoreType.DMA((count,)) for count in sems],
        compiler_params=pltpu.CompilerParams(collective_id=0, has_side_effects=True),
        name="opening",
    )(*weights, *tokens)


def pairs_of(section, shift, n):
    return [(section * n + i, section * n + (i + shift) % n) for i in range(n)]


def row_scatter(term, axis, section):
    n = lax.axis_size("row")
    other = lax.ppermute(term.astype(BF16), "section", [(1 - section, section)])
    total = term + other.astype(F32)
    if n > 8:
        return lax.psum_scatter(
            total.astype(BF16), "row", scatter_dimension=axis, tiled=True
        ).astype(F32)
    me = lax.axis_index("row")
    sizes = tuple(d // n if a == axis else d for a, d in enumerate(term.shape))

    def chunk(k):
        at = lax.rem(me + k, n) * sizes[axis]
        return lax.dynamic_slice(total, (at, 0) if axis == 0 else (0, at), sizes)

    arrived = [
        lax.ppermute(chunk(k).astype(BF16), ("section", "row"), pairs_of(section, k, n))
        for k in range(1, n)
    ]
    result = chunk(0)
    for piece in arrived:
        result = result + piece.astype(F32)
    return result


def rotary_tables(length, heads):
    places = jnp.arange(length).astype(F32)
    inverse = 10000.0 ** (-jnp.arange(0, ROT, 2).astype(F32) / ROT)
    angles = places[:, None] * inverse[None, :]
    cosine, sine = jnp.cos(angles), jnp.sin(angles)
    half = ROT // 2
    ones = jnp.ones((length, HD - ROT), F32)
    zeros = jnp.zeros((length, HD - ROT), F32)
    nil = jnp.zeros((length, half), F32)
    cos_one = jnp.concatenate([cosine, cosine, ones], axis=1)
    ahead_one = jnp.concatenate([-sine, nil, zeros], axis=1)
    behind_one = jnp.concatenate([nil, sine, zeros], axis=1)
    flat = jnp.zeros((length, HD), F32)

    def full(one, last):
        return jnp.tile(jnp.concatenate([one, one, last], axis=1), (1, heads))

    return full(cos_one, flat + 1.0), full(ahead_one, flat), full(behind_one, flat)


def shifted(array, by):
    return jnp.roll(array, by, axis=1)


def rotate(packed, tables):
    cosine, ahead, behind = tables
    half = ROT // 2
    return packed * cosine + shifted(packed, -half) * ahead + shifted(packed, half) * behind


def rotate_back(grad, tables):
    cosine, ahead, behind = tables
    half = ROT // 2
    return grad * cosine + shifted(grad * ahead, half) + shifted(grad * behind, -half)


def scores_of(query_block, keys_all, segment, begin, stop):
    places = jnp.arange(stop)
    scores = jnp.einsum(
        "qhd,khd->hqk", query_block, keys_all[:stop], preferred_element_type=F32
    ) * HD ** (-0.5)
    allowed = (segment[begin:stop, None] == segment[None, :stop]) & (
        places[begin:, None] >= places[None, :]
    )
    return jnp.where(allowed[None], scores, -1000000000.0)


def split_heads(packed):
    length, width = packed.shape
    parts = packed.reshape(length, width // (3 * HD), 3, HD)
    return parts[:, :, 0], parts[:, :, 1], parts[:, :, 2]


def attention_forward(packed, segment):
    queries, keys_all, values = split_heads(packed)
    length = packed.shape[0]
    block = min(512, length)
    outputs, totals = [], []
    for begin in range(0, length, block):
        stop = begin + block
        scores = scores_of(queries[begin:stop], keys_all, segment, begin, stop)
        biggest = jnp.max(scores, axis=-1, keepdims=True)
        raised = jnp.exp(scores - biggest)
        summed = jnp.sum(raised, axis=-1, keepdims=True)
        softened = (raised / summed).astype(BF16)
        outputs.append(
            jnp.einsum("hqk,khd->qhd", softened, values[:stop], preferred_element_type=F32)
        )
        totals.append((biggest + jnp.log(summed))[..., 0])
    context = jnp.concatenate(outputs, axis=0).astype(BF16).reshape(length, -1)
    return context, jnp.concatenate(totals, axis=1)


def attention_backward(packed, segment, log_totals, context_grad):
    queries, keys_all, values = split_heads(packed)
    length, heads = queries.shape[:2]
    context_grad = context_grad.reshape(length, heads, HD)
    block = min(512, length)
    factor = HD ** (-0.5)
    key_grad = jnp.zeros(keys_all.shape, F32)
    value_grad = jnp.zeros(values.shape, F32)
    query_grads = []
    for begin in range(0, length, block):
        stop = begin + block
        query_block = queries[begin:stop]
        grad_block = context_grad[begin:stop]
        scores = scores_of(query_block, keys_all, segment, begin, stop)
        softened = jnp.exp(scores - log_totals[:, begin:stop, None])
        soft_grad = jnp.einsum(
            "qhd,khd->hqk", grad_block, values[:stop], preferred_element_type=F32
        )
        inner = jnp.sum(softened * soft_grad, axis=-1, keepdims=True)
        score_grad = (softened * (soft_grad - inner)).astype(BF16)
        query_grads.append(
            jnp.einsum("hqk,khd->qhd", score_grad, keys_all[:stop], preferred_element_type=F32)
            * factor
        )
        key_grad = key_grad.at[:stop].add(
            jnp.einsum("hqk,qhd->khd", score_grad, query_block, preferred_element_type=F32)
            * factor
        )
        value_grad = value_grad.at[:stop].add(
            jnp.einsum(
                "hqk,qhd->khd", softened.astype(BF16), grad_block, preferred_element_type=F32
            )
        )
    grads = jnp.stack([jnp.concatenate(query_grads, axis=0), key_grad, value_grad], axis=2)
    return grads.reshape(length, -1)


def normalize(inputs):
    values_in = inputs.astype(F32)
    centre = jnp.mean(values_in, axis=1, keepdims=True)
    spread = jnp.mean(values_in * values_in, axis=1, keepdims=True) - centre * centre
    inverse = lax.rsqrt(spread + EPSILON)
    return (values_in - centre) * inverse, inverse


def layer_forward(own, inputs, segment, weights, gains, biases, tables):
    qkv, up, both = weights
    scaled = normalize(inputs)[0]
    attn_in = (scaled * gains[0] + biases[0]).astype(BF16)
    mlp_in = (scaled * gains[1] + biases[1]).astype(BF16)
    packed = rotate(jnp.dot(attn_in, qkv, preferred_element_type=F32), tables).astype(BF16)
    context, log_totals = attention_forward(packed, segment)
    hidden = jnp.dot(mlp_in, up, preferred_element_type=F32)
    active = jax.nn.gelu(hidden, approximate=False).astype(BF16)
    joined = jnp.concatenate([context, active], axis=1)
    branch = col_scatter(jnp.dot(joined, both, preferred_element_type=F32))
    result = (own.astype(F32) + branch).astype(BF16)
    return result, (own, inputs, attn_in, mlp_in, packed, log_totals, context)


def layer_backward(own_grad, grad_all, stored, segment, weights, gains, tables):
    qkv, up, both = weights
    own, inputs, attn_in, mlp_in, packed, log_totals, context = stored
    width = context.shape[1]
    joined_grad = contract(grad_all, both, 1, 1)
    context_grad = joined_grad[:, :width].astype(BF16)
    hidden = jnp.dot(mlp_in, up, preferred_element_type=F32)
    active, gelu_pull = jax.vjp(partial(jax.nn.gelu, approximate=False), hidden)
    hidden_grad = gelu_pull(joined_grad[:, width:])[0].astype(BF16)
    packed_grad = attention_backward(packed, segment, log_totals, context_grad)
    packed_grad = rotate_back(packed_grad, tables).astype(BF16)
    attn_grad = contract(packed_grad, qkv, 1, 1)
    mlp_grad = contract(hidden_grad, up, 1, 1)
    reduced = col_scatter(attn_grad * gains[0] + mlp_grad * gains[1])
    scaled_own, inverse_own = normalize(own)
    grad_mean = jnp.mean(reduced, axis=1, keepdims=True)
    cross_mean = jnp.mean(reduced * scaled_own, axis=1, keepdims=True)
    input_grad = own_grad.astype(F32) + inverse_own * (
        reduced - grad_mean - scaled_own * cross_mean
    )
    scaled = normalize(inputs)[0]
    small = jnp.stack(
        [
            jnp.sum(attn_grad * scaled, axis=0),
            jnp.sum(mlp_grad * scaled, axis=0),
            jnp.sum(attn_grad, axis=0),
            jnp.sum(mlp_grad, axis=0),
        ]
    )
    qkv_term = contract(attn_in, packed_grad, 0, 0)
    up_term = contract(mlp_in, hidden_grad, 0, 0)
    joined = jnp.concatenate([context, active.astype(BF16)], axis=1)
    both_term = contract(joined, grad_all, 0, 0)
    return input_grad.astype(BF16), (qkv_term, up_term, both_term), small


def butterfly(value, axis):
    n = lax.axis_size(axis)
    step = 1
    while step < n:
        value = value + lax.ppermute(value, axis, [(i, i ^ step) for i in range(n)])
        step *= 2
    return value


def body(acts, segments, norm_gains, norm_biases, w_qkv, w_out, w_up, w_down, out_grad):
    section = lax.axis_index("section")
    first = section == 0

    def mine(member):
        return lax.dynamic_index_in_dim(member, section, 0, keepdims=False)

    def swap(value):
        return lax.ppermute(value, "section", [(0, 1), (1, 0)])

    own = mine(acts)
    segment = mine(segments)
    last_grad = mine(out_grad)
    joined_local = jnp.concatenate([w_out[0], w_down[0]], axis=0)
    qkv_all, up_all, both_all, inputs, grad_all = opening(
        (w_qkv[0], w_up[0], joined_local), (own, last_grad)
    )
    width = own.shape[1]
    inputs, grad_all = inputs.reshape(-1, width), grad_all.reshape(-1, width)
    weights = [
        (
            qkv_all[layer].reshape(width, -1),
            up_all[layer].reshape(width, -1),
            both_all[layer].transpose(1, 0, 2).reshape(-1, width),
        )
        for layer in range(2)
    ]
    norms = jnp.concatenate([norm_gains[0], norm_biases[0]], axis=0)
    norms_other = swap(norms)
    layer_norms = [
        jnp.where(first, norms, norms_other),
        jnp.where(first, norms_other, norms),
    ]
    gains = [member[:2] for member in layer_norms]
    biases = [member[2:] for member in layer_norms]
    tables = rotary_tables(inputs.shape[0], w_qkv.shape[2] // (3 * HD))

    middle, stored_first = layer_forward(
        own, inputs, segment, weights[0], gains[0], biases[0], tables
    )
    inputs_last = col_gather(middle)
    last, stored_last = layer_forward(
        middle, inputs_last, segment, weights[1], gains[1], biases[1], tables
    )
    middle_grad, terms_last, small_last = layer_backward(
        last_grad, grad_all, stored_last, segment, weights[1], gains[1], tables
    )
    middle_grad_all = col_gather(middle_grad)
    totals_last = [row_scatter(t, a, 1) for t, a in zip(terms_last, (0, 0, 1))]
    first_grad, terms_first, small_first = layer_backward(
        middle_grad, middle_grad_all, stored_first, segment, weights[0], gains[0], tables
    )
    totals_first = [row_scatter(t, a, 0) for t, a in zip(terms_first, (0, 0, 1))]
    totals = [jnp.where(first, a, b) for a, b in zip(totals_first, totals_last)]

    small = jnp.where(first, small_first, small_last) + swap(
        jnp.where(first, small_last, small_first)
    )
    small = butterfly(butterfly(small, "col"), "row")

    def placed(of_first, of_last):
        kept = jnp.where(first, of_first, of_last)
        arrived = swap(jnp.where(first, of_last, of_first))
        return jnp.where(first, jnp.stack([kept, arrived]), jnp.stack([arrived, kept]))[None]

    split = w_out.shape[1]
    return (
        placed(middle, last),
        placed(first_grad, middle_grad),
        small[:2][None],
        small[2][None],
        small[3][None],
        totals[0][None],
        totals[2][:split][None],
        totals[1][None],
        totals[2][split:][None],
    )


def solution(mesh):
    placed = (
        P(None, ("row", "col"), None),
        P(None, "row"),
        P("section", None, None),
        P("section", None, None),
        P("section", "row", "col"),
        P("section", "col", "row"),
        P("section", "row", "col"),
        P("section", "col", "row"),
        P(None, ("row", "col"), None),
    )
    return jax.shard_map(
        body,
        mesh=mesh,
        in_specs=placed,
        out_specs=(
            P("section", None, ("row", "col"), None),
            P("section", None, ("row", "col"), None),
            P("section", None, None),
            P("section", None),
            P("section", None),
            P("section", "row", "col"),
            P("section", "col", "row"),
            P("section", "row", "col"),
            P("section", "col", "row"),
        ),
        check_vma=False,
    )
```

```python
from functools import partial

import jax
import jax.numpy as jnp
from jax import lax
from jax.experimental import pallas as pl
from jax.experimental.pallas import tpu as pltpu
from jax.sharding import PartitionSpec as P

HD = 64
ROT = 16
EPSILON = 1e-05
F32 = jnp.float32
BF16 = jnp.bfloat16


def contract(left, right, left_dim, right_dim):
    return lax.dot_general(
        left, right, (((left_dim,), (right_dim,)), ((), ())), preferred_element_type=F32
    )


def col_gather(piece):
    n = lax.axis_size("col")
    me = lax.axis_index("col")
    rows = piece.shape[0]
    pieces = [piece]
    for k in range(1, n):
        pieces.append(lax.ppermute(piece, "col", [(i, (i + k) % n) for i in range(n)]))
    whole = jnp.zeros((rows * n, piece.shape[1]), piece.dtype)
    for k in range(n):
        whole = lax.dynamic_update_slice(whole, pieces[k], (lax.rem(me - k + n, n) * rows, 0))
    return whole


def col_scatter(total):
    n = lax.axis_size("col")
    me = lax.axis_index("col")
    rows = total.shape[0] // n
    width = total.shape[1]
    low = total.astype(BF16)

    def chunk(source, k):
        return lax.dynamic_slice(source, (lax.rem(me + k, n) * rows, 0), (rows, width))

    arrived = [
        lax.ppermute(chunk(low, k), "col", [(i, (i + k) % n) for i in range(n)])
        for k in range(1, n)
    ]
    result = chunk(total, 0)
    for piece in arrived:
        result = result + piece.astype(F32)
    return result


def remote(source, target, send, recv, device):
    return pltpu.make_async_remote_copy(
        src_ref=source,
        dst_ref=target,
        send_sem=send,
        recv_sem=recv,
        device_id=device,
        device_id_type=pl.DeviceIdType.MESH,
    )


def greet(devices):
    barrier = pltpu.get_barrier_semaphore()
    for device in devices:
        pl.semaphore_signal(
            barrier, inc=1, device_id=device, device_id_type=pl.DeviceIdType.MESH
        )
    pl.semaphore_wait(barrier, len(devices))


def opening_kernel(nr, nc, *refs):
    pieces, outs = refs[:5], refs[5:10]
    local, row_send, row_recv, pair_send, pair_recv, col_send, col_recv = refs[10:]
    section, row, col = (lax.axis_index(a) for a in ("section", "row", "col"))
    partner = {"section": 1 - section}
    rows = [{"row": lax.rem(row + k, nr)} for k in range(1, nr)]
    cols = [{"col": lax.rem(col + k, nc)} for k in range(1, nc)]
    greet(rows + cols + [partner])
    weights, wholes = pieces[:3], outs[:3]
    tokens, gathered = pieces[3:], outs[3:]
    waits = []
    for k in range(1, nr):
        for j in range(3):
            copy = remote(
                weights[j],
                wholes[j].at[section, row],
                row_send.at[j * nr + k],
                row_recv.at[j * nr + k],
                rows[k - 1],
            )
            copy.start()
            waits.append(copy)
    for k in range(1, nc):
        for j in range(2):
            copy = remote(
                tokens[j],
                gathered[j].at[col],
                col_send.at[j * nc + k],
                col_recv.at[j * nc + k],
                cols[k - 1],
            )
            copy.start()
            waits.append(copy)
    locals_here = []
    passing = []
    for j in range(3):
        locals_here.append(
            pltpu.make_async_copy(weights[j], wholes[j].at[section, row], local.at[j])
        )
        passing.append(
            remote(
                weights[j],
                wholes[j].at[section, row],
                pair_send.at[j * nr],
                pair_recv.at[j * nr],
                partner,
            )
        )
    for j in range(2):
        locals_here.append(
            pltpu.make_async_copy(tokens[j], gathered[j].at[col], local.at[3 + j])
        )
    for copy in locals_here + passing:
        copy.start()
    for k in range(1, nr):
        origin = lax.rem(row - k + nr, nr)
        for j in range(3):
            waits[(k - 1) * 3 + j].wait_recv()
            copy = remote(
                wholes[j].at[section, origin],
                wholes[j].at[section, origin],
                pair_send.at[j * nr + k],
                pair_recv.at[j * nr + k],
                partner,
            )
            copy.start()
            passing.append(copy)
    for copy in locals_here:
        copy.wait()
    for at, copy in enumerate(waits):
        copy.wait_send()
        if at >= 3 * (nr - 1):
            copy.wait_recv()
    for copy in passing:
        copy.wait()


def opening(weights, tokens):
    nr, nc = lax.axis_size("row"), lax.axis_size("col")
    shapes = [jax.ShapeDtypeStruct((2, nr) + w.shape, w.dtype) for w in weights]
    shapes += [jax.ShapeDtypeStruct((nc,) + t.shape, t.dtype) for t in tokens]
    sems = [5, 3 * nr, 3 * nr, 3 * nr, 3 * nr, 2 * nc, 2 * nc]
    return pl.pallas_call(
        partial(opening_kernel, nr, nc),
        out_shape=shapes,
        in_specs=[pl.BlockSpec(memory_space=pl.ANY)] * 5,
        out_specs=[pl.BlockSpec(memory_space=pl.ANY)] * 5,
        scratch_shapes=[pltpu.SemaphoreType.DMA((count,)) for count in sems],
        compiler_params=pltpu.CompilerParams(collective_id=0, has_side_effects=True),
        name="opening",
    )(*weights, *tokens)


def closing_kernel(nr, *refs):
    pieces, outs, send, recv = refs[:4], refs[4:8], refs[8], refs[9]
    row = lax.axis_index("row")
    targets = [lax.rem(row + k, nr) for k in range(1, nr)]
    greet([{"row": target} for target in targets])
    copies = []
    for k in range(1, nr):
        target = targets[k - 1]
        for j in range(4):
            copy = remote(
                pieces[j] if j == 3 else pieces[j].at[target],
                outs[j].at[k - 1],
                send.at[j * nr + k],
                recv.at[j * nr + k],
                {"row": target},
            )
            copy.start()
            copies.append(copy)
    for copy in copies:
        copy.wait()


def closing(totals, small):
    nr = lax.axis_size("row")
    row = lax.axis_index("row")
    low = [total.astype(BF16) for total in totals]
    shapes = [jax.ShapeDtypeStruct((nr - 1,) + t.shape[1:], BF16) for t in low]
    shapes.append(jax.ShapeDtypeStruct((nr - 1,) + small.shape, F32))
    arrived = pl.pallas_call(
        partial(closing_kernel, nr),
        out_shape=shapes,
        in_specs=[pl.BlockSpec(memory_space=pl.ANY)] * 4,
        out_specs=[pl.BlockSpec(memory_space=pl.ANY)] * 4,
        scratch_shapes=[pltpu.SemaphoreType.DMA((4 * nr,)) for _ in range(2)],
        compiler_params=pltpu.CompilerParams(collective_id=1, has_side_effects=True),
        name="closing",
    )(*low, small)
    results = [
        lax.dynamic_index_in_dim(total, row, 0, keepdims=False)
        + jnp.sum(pieces.astype(F32), axis=0)
        for total, pieces in zip(totals, arrived)
    ]
    return results, small + jnp.sum(arrived[3], axis=0)


def rotary_tables(length, heads):
    places = jnp.arange(length).astype(F32)
    inverse = 10000.0 ** (-jnp.arange(0, ROT, 2).astype(F32) / ROT)
    angles = places[:, None] * inverse[None, :]
    cosine, sine = jnp.cos(angles), jnp.sin(angles)
    half = ROT // 2
    ones = jnp.ones((length, HD - ROT), F32)
    zeros = jnp.zeros((length, HD - ROT), F32)
    nil = jnp.zeros((length, half), F32)
    cos_one = jnp.concatenate([cosine, cosine, ones], axis=1)
    ahead_one = jnp.concatenate([-sine, nil, zeros], axis=1)
    behind_one = jnp.concatenate([nil, sine, zeros], axis=1)
    flat = jnp.zeros((length, HD), F32)

    def full(one, last):
        return jnp.tile(jnp.concatenate([one, one, last], axis=1), (1, heads))

    return full(cos_one, flat + 1.0), full(ahead_one, flat), full(behind_one, flat)


def shifted(array, by):
    return jnp.roll(array, by, axis=1)


def rotate(packed, tables):
    cosine, ahead, behind = tables
    half = ROT // 2
    return packed * cosine + shifted(packed, -half) * ahead + shifted(packed, half) * behind


def rotate_back(grad, tables):
    cosine, ahead, behind = tables
    half = ROT // 2
    return grad * cosine + shifted(grad * ahead, half) + shifted(grad * behind, -half)


def scores_of(query_block, keys_all, segment, begin, stop):
    places = jnp.arange(stop)
    scores = jnp.einsum(
        "qhd,khd->hqk", query_block, keys_all[:stop], preferred_element_type=F32
    ) * HD ** (-0.5)
    allowed = (segment[begin:stop, None] == segment[None, :stop]) & (
        places[begin:, None] >= places[None, :]
    )
    return jnp.where(allowed[None], scores, -1000000000.0)


def split_heads(packed):
    length, width = packed.shape
    parts = packed.reshape(length, width // (3 * HD), 3, HD)
    return parts[:, :, 0], parts[:, :, 1], parts[:, :, 2]


def attention_forward(packed, segment):
    queries, keys_all, values = split_heads(packed)
    length = packed.shape[0]
    block = min(512, length)
    outputs, totals = [], []
    for begin in range(0, length, block):
        stop = begin + block
        scores = scores_of(queries[begin:stop], keys_all, segment, begin, stop)
        biggest = jnp.max(scores, axis=-1, keepdims=True)
        raised = jnp.exp(scores - biggest)
        summed = jnp.sum(raised, axis=-1, keepdims=True)
        softened = (raised / summed).astype(BF16)
        outputs.append(
            jnp.einsum("hqk,khd->qhd", softened, values[:stop], preferred_element_type=F32)
        )
        totals.append((biggest + jnp.log(summed))[..., 0])
    context = jnp.concatenate(outputs, axis=0).astype(BF16).reshape(length, -1)
    return context, jnp.concatenate(totals, axis=1)


def attention_backward(packed, segment, log_totals, context_grad):
    queries, keys_all, values = split_heads(packed)
    length, heads = queries.shape[:2]
    context_grad = context_grad.reshape(length, heads, HD)
    block = min(512, length)
    factor = HD ** (-0.5)
    key_grad = jnp.zeros(keys_all.shape, F32)
    value_grad = jnp.zeros(values.shape, F32)
    query_grads = []
    for begin in range(0, length, block):
        stop = begin + block
        query_block = queries[begin:stop]
        grad_block = context_grad[begin:stop]
        scores = scores_of(query_block, keys_all, segment, begin, stop)
        softened = jnp.exp(scores - log_totals[:, begin:stop, None])
        soft_grad = jnp.einsum(
            "qhd,khd->hqk", grad_block, values[:stop], preferred_element_type=F32
        )
        inner = jnp.sum(softened * soft_grad, axis=-1, keepdims=True)
        score_grad = (softened * (soft_grad - inner)).astype(BF16)
        query_grads.append(
            jnp.einsum("hqk,khd->qhd", score_grad, keys_all[:stop], preferred_element_type=F32)
            * factor
        )
        key_grad = key_grad.at[:stop].add(
            jnp.einsum("hqk,qhd->khd", score_grad, query_block, preferred_element_type=F32)
            * factor
        )
        value_grad = value_grad.at[:stop].add(
            jnp.einsum(
                "hqk,qhd->khd", softened.astype(BF16), grad_block, preferred_element_type=F32
            )
        )
    grads = jnp.stack([jnp.concatenate(query_grads, axis=0), key_grad, value_grad], axis=2)
    return grads.reshape(length, -1)


def normalize(inputs):
    values_in = inputs.astype(F32)
    centre = jnp.mean(values_in, axis=1, keepdims=True)
    spread = jnp.mean(values_in * values_in, axis=1, keepdims=True) - centre * centre
    inverse = lax.rsqrt(spread + EPSILON)
    return (values_in - centre) * inverse, inverse


def layer_forward(own, inputs, segment, weights, gains, biases, tables):
    qkv, up, both = weights
    scaled = normalize(inputs)[0]
    attn_in = (scaled * gains[0] + biases[0]).astype(BF16)
    mlp_in = (scaled * gains[1] + biases[1]).astype(BF16)
    packed = rotate(jnp.dot(attn_in, qkv, preferred_element_type=F32), tables).astype(BF16)
    context, log_totals = attention_forward(packed, segment)
    hidden = jnp.dot(mlp_in, up, preferred_element_type=F32)
    active = jax.nn.gelu(hidden, approximate=False).astype(BF16)
    joined = jnp.concatenate([context, active], axis=1)
    branch = col_scatter(jnp.dot(joined, both, preferred_element_type=F32))
    result = (own.astype(F32) + branch).astype(BF16)
    return result, (own, inputs, attn_in, mlp_in, packed, log_totals, context)


def layer_backward(own_grad, grad_all, stored, segment, weights, gains, tables):
    qkv, up, both = weights
    own, inputs, attn_in, mlp_in, packed, log_totals, context = stored
    width = context.shape[1]
    joined_grad = contract(grad_all, both, 1, 1)
    context_grad = joined_grad[:, :width].astype(BF16)
    hidden = jnp.dot(mlp_in, up, preferred_element_type=F32)
    active, gelu_pull = jax.vjp(partial(jax.nn.gelu, approximate=False), hidden)
    hidden_grad = gelu_pull(joined_grad[:, width:])[0].astype(BF16)
    packed_grad = attention_backward(packed, segment, log_totals, context_grad)
    packed_grad = rotate_back(packed_grad, tables).astype(BF16)
    attn_grad = contract(packed_grad, qkv, 1, 1)
    mlp_grad = contract(hidden_grad, up, 1, 1)
    reduced = col_scatter(attn_grad * gains[0] + mlp_grad * gains[1])
    scaled_own, inverse_own = normalize(own)
    grad_mean = jnp.mean(reduced, axis=1, keepdims=True)
    cross_mean = jnp.mean(reduced * scaled_own, axis=1, keepdims=True)
    input_grad = own_grad.astype(F32) + inverse_own * (
        reduced - grad_mean - scaled_own * cross_mean
    )
    scaled = normalize(inputs)[0]
    small = jnp.stack(
        [
            jnp.sum(attn_grad * scaled, axis=0),
            jnp.sum(mlp_grad * scaled, axis=0),
            jnp.sum(attn_grad, axis=0),
            jnp.sum(mlp_grad, axis=0),
        ]
    )
    qkv_term = contract(attn_in, packed_grad, 0, 0)
    up_term = contract(mlp_in, hidden_grad, 0, 0)
    joined = jnp.concatenate([context, active.astype(BF16)], axis=1)
    both_term = contract(joined, grad_all, 0, 0)
    return input_grad.astype(BF16), (qkv_term, up_term, both_term), small


def butterfly(value, axis):
    n = lax.axis_size(axis)
    step = 1
    while step < n:
        value = value + lax.ppermute(value, axis, [(i, i ^ step) for i in range(n)])
        step *= 2
    return value


def body(acts, segments, norm_gains, norm_biases, w_qkv, w_out, w_up, w_down, out_grad):
    section = lax.axis_index("section")
    first = section == 0

    def mine(member):
        return lax.dynamic_index_in_dim(member, section, 0, keepdims=False)

    def swap(value):
        return lax.ppermute(value, "section", [(0, 1), (1, 0)])

    own = mine(acts)
    segment = mine(segments)
    last_grad = mine(out_grad)
    joined_local = jnp.concatenate([w_out[0], w_down[0]], axis=0)
    qkv_all, up_all, both_all, inputs, grad_all = opening(
        (w_qkv[0], w_up[0], joined_local), (own, last_grad)
    )
    width = own.shape[1]
    inputs, grad_all = inputs.reshape(-1, width), grad_all.reshape(-1, width)
    weights = [
        (
            qkv_all[layer].reshape(width, -1),
            up_all[layer].reshape(width, -1),
            both_all[layer].transpose(1, 0, 2).reshape(-1, width),
        )
        for layer in range(2)
    ]
    norms = jnp.concatenate([norm_gains[0], norm_biases[0]], axis=0)
    norms_other = swap(norms)
    layer_norms = [
        jnp.where(first, norms, norms_other),
        jnp.where(first, norms_other, norms),
    ]
    gains = [member[:2] for member in layer_norms]
    biases = [member[2:] for member in layer_norms]
    tables = rotary_tables(inputs.shape[0], w_qkv.shape[2] // (3 * HD))

    middle, stored_first = layer_forward(
        own, inputs, segment, weights[0], gains[0], biases[0], tables
    )
    inputs_last = col_gather(middle)
    last, stored_last = layer_forward(
        middle, inputs_last, segment, weights[1], gains[1], biases[1], tables
    )
    middle_grad, terms_last, small_last = layer_backward(
        last_grad, grad_all, stored_last, segment, weights[1], gains[1], tables
    )
    middle_grad_all = col_gather(middle_grad)
    nr = lax.axis_size("row")

    def to_section(terms, layer):
        return [lax.ppermute(t.astype(BF16), "section", [(1 - layer, layer)]) for t in terms]

    others_last = to_section(terms_last, 1)
    first_grad, terms_first, small_first = layer_backward(
        middle_grad, middle_grad_all, stored_first, segment, weights[0], gains[0], tables
    )
    others_first = to_section(terms_first, 0)
    small = jnp.where(first, small_first, small_last) + swap(
        jnp.where(first, small_last, small_first)
    )
    small = butterfly(small, "col")
    totals = [
        jnp.where(first, a, b) + jnp.where(first, c, d).astype(F32)
        for a, b, c, d in zip(terms_first, terms_last, others_first, others_last)
    ]
    qkv_total, up_total, both_total = totals
    totals, small = closing(
        (
            qkv_total.reshape(nr, -1, qkv_total.shape[1]),
            up_total.reshape(nr, -1, up_total.shape[1]),
            both_total.reshape(both_total.shape[0], nr, -1).transpose(1, 0, 2),
        ),
        small,
    )

    def placed(of_first, of_last):
        kept = jnp.where(first, of_first, of_last)
        arrived = swap(jnp.where(first, of_last, of_first))
        return jnp.where(first, jnp.stack([kept, arrived]), jnp.stack([arrived, kept]))[None]

    split = w_out.shape[1]
    return (
        placed(middle, last),
        placed(first_grad, middle_grad),
        small[:2][None],
        small[2][None],
        small[3][None],
        totals[0][None],
        totals[2][:split][None],
        totals[1][None],
        totals[2][split:][None],
    )


def solution(mesh):
    placed = (
        P(None, ("row", "col"), None),
        P(None, "row"),
        P("section", None, None),
        P("section", None, None),
        P("section", "row", "col"),
        P("section", "col", "row"),
        P("section", "row", "col"),
        P("section", "col", "row"),
        P(None, ("row", "col"), None),
    )
    return jax.shard_map(
        body,
        mesh=mesh,
        in_specs=placed,
        out_specs=(
            P("section", None, ("row", "col"), None),
            P("section", None, ("row", "col"), None),
            P("section", None, None),
            P("section", None),
            P("section", None),
            P("section", "row", "col"),
            P("section", "col", "row"),
            P("section", "row", "col"),
            P("section", "col", "row"),
        ),
        check_vma=False,
    )
```
